32 devices in a mesh: ctx: 4 (over y, core), tp: 8 (over z, x).
Axes of the slice: x: 2, y: 2, z: 4, core: 2. Of those that a mesh axis runs over, the one named last changes fastest.
Arguments:
- query_in: bfloat16 [4096, 8192], P('ctx', 'tp'), may hold values from -6 to 6
- key_in: bfloat16 [4096, 8192], P('ctx', 'tp'), may hold values from -6 to 6
- value_in: bfloat16 [4096, 8192], P('ctx', 'tp'), may hold values from -6 to 6
- short_taps: float32 [3, 7, 8192], P(None, None, 'tp'), may hold values from -2 to 2
- modal_poles: float32 [16, 8192], P(None, 'tp'), may hold values from 0 to 1, as said below
- modal_residues: float32 [16, 8192], P(None, 'tp'), may hold values from -0.5 to 0.5
- out_weight: bfloat16 [8192, 8192], P('tp'), may hold values from -0.0625 to 0.0625
- grad_out: bfloat16 [4096, 8192], P('ctx', 'tp'), may hold values from -6 to 6
Outputs:
- gated: bfloat16 [4096, 8192], P('ctx', 'tp')
- grad_query: bfloat16 [4096, 8192], P('ctx', 'tp')
- grad_key: bfloat16 [4096, 8192], P('ctx', 'tp')
- grad_value: bfloat16 [4096, 8192], P('ctx', 'tp')
The draws below stay inside these ranges and needn't reach their ends.
Inputs may be any that keep to these rules, and one draw needn't show every extreme that they name: `modal_poles`: every pole lies strictly between 0 and 1.
All inputs are finite; a program needn't handle non-finite values.
Results may differ from the reference program's by a relative error of at most 0.0017.
Values may be sent and summed in bfloat16 or wider, within the bound.
A program may use at most 192 MiB of HBM per device.

```python
import math
import jax
import jax.numpy as jnp
from jax import lax

D = 8192
MODES = 16
TAPS = 7
SEQ = 4096


def pole_rates(key, slow_share):
    key = jax.random.fold_in(key, 7)
    pick_key, slow_key, fast_key = jax.random.split(key, 3)
    shape = (MODES, D)
    slow_rate = jnp.exp(jax.random.uniform(slow_key, shape, jnp.float32, math.log(0.2 / SEQ), math.log(2.0 / SEQ)))
    fast_rate = jnp.exp(jax.random.uniform(fast_key, shape, jnp.float32, math.log(2.0 / SEQ), math.log(1.0 / 30.0)))
    chosen = jnp.where(jax.random.uniform(pick_key, shape) < slow_share, slow_rate, fast_rate)
    return jnp.exp(-chosen)


def draw_modal_poles(key, part):
    share = 0.5
    return pole_rates(key, share).astype(jnp.float32)


def draw_modal_residues(key, part):
    share = 0.5
    poles_drawn = pole_rates(key, share)
    key = jax.random.fold_in(key, 3)
    normal_part = jnp.clip(jax.random.normal(key, (MODES, D), jnp.float32), -4.0, 4.0)
    return (0.35 * normal_part * jnp.sqrt(1.0 - poles_drawn * poles_drawn)).astype(jnp.float32)


def levels(rng, extent, cuts, low, high):
    gain = 1.0
    for position, parts in cuts:
        draws = jax.random.uniform(jax.random.fold_in(jax.random.fold_in(rng, 6), position), (parts,), jnp.float32, low / len(cuts), high / len(cuts))
        gain = gain * jnp.repeat(jnp.exp(draws), extent[position] // parts).reshape((-1,) + (1,) * (len(extent) - 1 - position))
    return gain


def scatter_about(rng, extent, spread, most, cuts=(), kind=jnp.bfloat16):
    entries = spread * jax.random.normal(rng, extent, jnp.float32)
    if cuts:
        entries = entries * levels(rng, extent, cuts, -0.22, 0.18)
    return jnp.clip(entries, -most, most).astype(kind)


def setup_inputs(seed: int = 0) -> dict:
    seeds = jax.random.split(jax.random.key(seed), 9)
    query_in = scatter_about(seeds[0], (SEQ, D), 1.0, 6.0, ((0, 4), (1, 8)))
    key_in = scatter_about(seeds[1], (SEQ, D), 1.0, 6.0, ((0, 4), (1, 8)))
    value_in = scatter_about(seeds[2], (SEQ, D), 1.0, 6.0, ((0, 4), (1, 8)))
    short_taps = scatter_about(seeds[3], (3, TAPS, D), 0.4, 2.0, ((2, 8),), jnp.float32)
    modal_poles = draw_modal_poles(jax.random.fold_in(seeds[8], 71), 0)
    modal_residues = draw_modal_residues(jax.random.fold_in(seeds[8], 71), 0)
    out_weight = scatter_about(seeds[6], (D, D), D ** -0.5, 0.0625, ((0, 8),))
    grad_out = scatter_about(seeds[7], (SEQ, D), 1.0, 6.0, ((0, 4), (1, 8)))
    return {"query_in": query_in, "key_in": key_in, "value_in": value_in, "short_taps": short_taps, "modal_poles": modal_poles, "modal_residues": modal_residues, "out_weight": out_weight, "grad_out": grad_out}


def short_forward(signal, tap_rows):
    tap_count = tap_rows.shape[0]
    padded = jnp.pad(signal, ((tap_count - 1, 0), (0, 0)))
    summed = jnp.zeros_like(signal)
    for tap_index in range(tap_count):
        begin = tap_count - 1 - tap_index
        summed = summed + tap_rows[tap_index][None, :] * padded[begin:begin + SEQ]
    return summed


def short_backward(signal, tap_rows):
    tap_count = tap_rows.shape[0]
    padded = jnp.pad(signal, ((0, tap_count - 1), (0, 0)))
    summed = jnp.zeros_like(signal)
    for tap_index in range(tap_count):
        summed = summed + tap_rows[tap_index][None, :] * padded[tap_index:tap_index + SEQ]
    return summed


def modal_pass(signal, modal_poles, modal_residues, backward):
    def advance(state, row):
        state = modal_poles * state + row[None, :]
        return state, jnp.sum(modal_residues * state, axis=0)

    _, result = lax.scan(advance, jnp.zeros_like(modal_poles), signal, reverse=backward)
    return result


def reference(query_in, key_in, value_in, short_taps, modal_poles, modal_residues, out_weight, grad_out):
    q_short = short_forward(query_in.astype(jnp.float32), short_taps[0])
    k_short = short_forward(key_in.astype(jnp.float32), short_taps[1])
    v_short = short_forward(value_in.astype(jnp.float32), short_taps[2])
    product = k_short * v_short
    long_out = modal_pass(product, modal_poles, modal_residues, False)
    gated = (q_short * long_out).astype(jnp.bfloat16)
    grad_mixed = jnp.dot(grad_out, out_weight.T, preferred_element_type=jnp.float32)
    grad_qs = grad_mixed * long_out
    grad_long = grad_mixed * q_short
    grad_product = modal_pass(grad_long, modal_poles, modal_residues, True)
    grad_ks = grad_product * v_short
    grad_vs = grad_product * k_short
    grad_query = short_backward(grad_qs, short_taps[0]).astype(jnp.bfloat16)
    grad_key = short_backward(grad_ks, short_taps[1]).astype(jnp.bfloat16)
    grad_value = short_backward(grad_vs, short_taps[2]).astype(jnp.bfloat16)
    return (gated, grad_query, grad_key, grad_value)
```

```python
import jax
import jax.numpy as jnp
from jax import lax
from jax.experimental import pallas as pl
from jax.experimental.pallas import tpu as pltpu
from jax.sharding import PartitionSpec as P

LANES = 128
SEGS = 8
UNROLL = 8
HALO = 16
CHUNKS = 4
MESH = pl.DeviceIdType.MESH
F32 = jnp.float32


def from_behind(block, axis, distance):
    devices = range(lax.axis_size(axis))
    route = [(i - distance, i) for i in devices if i - distance in devices]
    return lax.ppermute(block, axis, route)


def power(base, exponent):
    result = None
    while exponent:
        if exponent & 1:
            result = base if result is None else result * base
        exponent >>= 1
        if exponent:
            base = base * base
    return result


def spread(row):
    return jnp.broadcast_to(row, (SEGS, LANES))


def tree_sum(terms):
    while len(terms) > 1:
        paired = [a + b for a, b in zip(terms[::2], terms[1::2])]
        terms = paired + ([terms[-1]] if len(terms) % 2 else [])
    return terms[0]


def short_pass(load, store, taps, steps, history):
    def body(outer, past):
        past = list(past)
        for inner in range(UNROLL):
            step = outer * UNROLL + inner
            past = [load(step)] + past
            store(step, tree_sum([tap * row for tap, row in zip(taps, past)]))
            past = past[: len(taps) - 1]
        return tuple(past)

    lax.fori_loop(0, steps // UNROLL, body, tuple(history))


def forward_ends(
    q_ref, k_ref, v_ref, prior_ref, taps_ref, poles_ref,
    qs_ref, ks_ref, vs_ref, ends_ref, own_ref, wide,
):
    steps, tok_rows = qs_ref.shape[0], q_ref.shape[0]
    modes, tap_count = poles_ref.shape[0], taps_ref.shape[1]
    for which, (source, target) in enumerate(((q_ref, qs_ref), (k_ref, ks_ref), (v_ref, vs_ref))):
        wide[0:HALO, :] = prior_ref[which].astype(F32)
        wide[HALO : HALO + tok_rows, :] = source[...].astype(F32)
        taps = [spread(taps_ref[which, j : j + 1, :]) for j in range(tap_count)]

        def load(step):
            return wide[pl.ds(HALO + step, SEGS, stride=steps), :]

        def store(step, value, target=target):
            target[step] = value

        short_pass(load, store, taps, steps, [load(-1 - j) for j in range(tap_count - 1)])
    poles = [spread(poles_ref[m : m + 1, :]) for m in range(modes)]

    def body(outer, states):
        for inner in range(UNROLL):
            step = outer * UNROLL + inner
            row = ks_ref[step] * vs_ref[step]
            states = tuple(p * s + row for p, s in zip(poles, states))
        return states

    zero = jnp.zeros((SEGS, LANES), F32)
    states = lax.fori_loop(0, steps // UNROLL, body, (zero,) * modes)
    for m in range(modes):
        ends_ref[m] = states[m]
    seg_decay = power(poles_ref[...], steps)
    run = ends_ref[:, 0, :]
    for seg in range(1, SEGS):
        run = seg_decay * run + ends_ref[:, seg, :]
    own_ref[...] = run


def entering(mine, gathered_ref, ends_ref, poles_ref, starts, steps, backward):
    count = gathered_ref.shape[0]
    seg_decay = power(poles_ref[...], steps)
    block_decay = power(seg_decay, SEGS)
    run = jnp.zeros_like(seg_decay)
    order = range(count)
    for k in reversed(order) if backward else order:
        keep = (k > mine) if backward else (k < mine)
        run = jnp.where(keep, block_decay * run + gathered_ref[k], run)
    segs = range(SEGS)
    for seg in reversed(segs) if backward else segs:
        starts[:, seg, :] = run
        run = seg_decay * run + ends_ref[:, seg, :]


def forward_out(
    mine, ks_ref, vs_ref, ends_ref, gathered_ref, poles_ref, residues_ref, long_ref, starts,
):
    steps = ks_ref.shape[0]
    modes = poles_ref.shape[0]
    entering(mine, gathered_ref, ends_ref, poles_ref, starts, steps, False)
    poles = [spread(poles_ref[m : m + 1, :]) for m in range(modes)]
    residues = [spread(residues_ref[m : m + 1, :]) for m in range(modes)]

    def body(outer, states):
        for inner in range(UNROLL):
            step = outer * UNROLL + inner
            row = ks_ref[step] * vs_ref[step]
            states = tuple(p * s + row for p, s in zip(poles, states))
            out = tree_sum([r * s for r, s in zip(residues, states)])
            long_ref[step] = out
        return states

    lax.fori_loop(0, steps // UNROLL, body, tuple(starts[m] for m in range(modes)))


def backward_ends(mixed_ref, qs_ref, poles_ref, ends_ref, own_ref, wide):
    steps, tok_rows = qs_ref.shape[0], mixed_ref.shape[0]
    modes = poles_ref.shape[0]
    poles = [spread(poles_ref[m : m + 1, :]) for m in range(modes)]
    wide[0:tok_rows, :] = mixed_ref[...]

    def body(outer, states):
        for inner in range(UNROLL):
            step = steps - 1 - (outer * UNROLL + inner)
            row = wide[pl.ds(step, SEGS, stride=steps), :] * qs_ref[step]
            states = tuple(p * s + row for p, s in zip(poles, states))
        return states

    zero = jnp.zeros((SEGS, LANES), F32)
    states = lax.fori_loop(0, steps // UNROLL, body, (zero,) * modes)
    for m in range(modes):
        ends_ref[m] = states[m]
    seg_decay = power(poles_ref[...], steps)
    run = ends_ref[:, SEGS - 1, :]
    for seg in reversed(range(SEGS - 1)):
        run = seg_decay * run + ends_ref[:, seg, :]
    own_ref[...] = run


def backward_out(
    mine_ref, mixed_ref, qs_ref, ks_ref, vs_ref, long_ref, ends_ref, gathered_ref,
    taps_ref, poles_ref, residues_ref,
    gated_ref, gq_ref, gk_ref, gv_ref, heads_ref, tails_ref, starts, grads, wide,
):
    steps, tok_rows = qs_ref.shape[0], mixed_ref.shape[0]
    modes, tap_count = poles_ref.shape[0], taps_ref.shape[1]
    rim = tap_count - 1
    entering(mine_ref[0], gathered_ref, ends_ref, poles_ref, starts, steps, True)
    poles = [spread(poles_ref[m : m + 1, :]) for m in range(modes)]
    residues = [spread(residues_ref[m : m + 1, :]) for m in range(modes)]

    def body(outer, states):
        for inner in range(UNROLL):
            step = steps - 1 - (outer * UNROLL + inner)
            mixed = mixed_ref[pl.ds(step, SEGS, stride=steps), :]
            q_row, long_row = qs_ref[step], long_ref[step]
            row = mixed * q_row
            states = tuple(p * s + row for p, s in zip(poles, states))
            out = tree_sum([r * s for r, s in zip(residues, states)])
            grads[0, step] = mixed * long_row
            wide[pl.ds(step, SEGS, stride=steps), :] = q_row * long_row
            grads[1, step] = out * vs_ref[step]
            grads[2, step] = out * ks_ref[step]
        return states

    lax.fori_loop(0, steps // UNROLL, body, tuple(starts[m] for m in range(modes)))
    gated_ref[...] = wide[...].astype(jnp.bfloat16)
    zero_row = jnp.zeros((1, LANES), F32)
    for which, target in enumerate((gq_ref, gk_ref, gv_ref)):
        heads_ref[which] = grads[which, 0:8, 0, :]
        later = [
            jnp.concatenate([grads[which, j][1:], zero_row], axis=0) for j in range(rim)
        ]
        taps = [spread(taps_ref[which, j : j + 1, :]) for j in range(tap_count)]

        def load(step, which=which):
            return grads[which, steps - 1 - step]

        def store(step, value):
            wide[pl.ds(steps - 1 - step, SEGS, stride=steps), :] = value

        short_pass(load, store, taps, steps, later)
        tails_ref[which] = wide[tok_rows - 8 :, :]
        target[...] = wide[...].astype(jnp.bfloat16)


def own_plane(tp):
    z, x = tp // 2, tp % 2
    low = z < 2
    place = jnp.where(low, z, 3 - z)

    def shard(p, column):
        return jnp.where(low, p, 3 - p) * 2 + column

    return place, x, shard


def gather_and_multiply(
    grad_ref, weight_ref, q_ref, k_ref, v_ref, taps_ref, poles_ref, residues_ref,
    mixed_ref, qs_ref, ks_ref, vs_ref, long_ref, back_ref, gathered_back_ref,
    got, tiles, halo, wide, ends, own, gathered, starts,
    send_sem, recv_sem, tile_sem, mine_sem, halo_send, halo_recv, state_send, state_recv,
):
    count = lax.axis_size("ctx")
    mine = lax.axis_index("ctx")
    tp = lax.axis_index("tp")
    place, x, shard = own_plane(tp)
    is_end = place == 0
    is_mid = place == 1
    tok_rows, chan = mixed_ref.shape
    feat = grad_ref.shape[1]
    part = tok_rows // CHUNKS
    half = CHUNKS // 2
    inward, outward, across = shard(place + 1, x), shard(place - 1, x), shard(place, 1 - x)

    barrier = pltpu.get_barrier_semaphore()
    greeted = jnp.where(is_end, shard(3, x), outward)
    for peer in (inward, across, greeted):
        pl.semaphore_signal(barrier, inc=1, device_id={"tp": peer}, device_id_type=MESH)
    for gap in range(1, count):
        other = lax.rem(mine + gap, count)
        pl.semaphore_signal(barrier, inc=1, device_id={"ctx": other}, device_id_type=MESH)
    pl.semaphore_wait(barrier, count + 2)

    def rows(c):
        return pl.ds(pl.multiple_of(c * part, part), part)

    def copy(slot, c, way, source=None):
        piece = got.at[slot, rows(c), :]
        return pltpu.make_async_remote_copy(
            src_ref=piece if source is None else source.at[rows(c), :],
            dst_ref=piece,
            send_sem=send_sem.at[way, slot, c],
            recv_sem=recv_sem.at[slot, c],
            device_id={"tp": (inward, outward, across)[way]},
            device_id_type=MESH,
        )

    def tile(slot, buffer):
        columns = pl.ds(pl.multiple_of(slot * feat, feat), feat)
        return pltpu.make_async_copy(
            weight_ref.at[:, columns], tiles.at[buffer], tile_sem.at[buffer]
        )

    def halo_copy(which):
        source = (q_ref, k_ref, v_ref)[which]
        return pltpu.make_async_remote_copy(
            src_ref=source.at[pl.ds(tok_rows - HALO, HALO), :],
            dst_ref=halo.at[which],
            send_sem=halo_send.at[which],
            recv_sem=halo_recv.at[which],
            device_id={"ctx": lax.rem(mine + 1, count)},
            device_id_type=MESH,
        )

    def state_copy(gap, way, landing):
        return pltpu.make_async_remote_copy(
            src_ref=own.at[way],
            dst_ref=landing.at[mine],
            send_sem=state_send.at[way, gap],
            recv_sem=state_recv.at[way, gap],
            device_id={"ctx": lax.rem(mine + gap, count)},
            device_id_type=MESH,
        )

    def state_exchange(way, landing):
        landing[mine] = own[way]
        for gap in range(1, count):
            state_copy(gap, way, landing).start()

    def state_wait(way, landing):
        for gap in range(1, count):
            state_copy(gap, way, landing).wait()

    def pair(k, end_slot, mid_slot):
        return jnp.where(is_end, end_slot, mid_slot)

    order = (
        tp,
        shard(place + 1, x),
        pair(2, shard(0, 1 - x), shard(0, x)),
        shard(place + 2, x),
        pair(4, shard(3, x), shard(1, 1 - x)),
        pair(5, shard(2, 1 - x), shard(0, 1 - x)),
        pair(6, shard(1, 1 - x), shard(2, 1 - x)),
        shard(3, 1 - x),
    )

    def pick(k):
        slot = order[7]
        for i in range(7):
            slot = jnp.where(k == i, order[i], slot)
        return slot

    for c in range(CHUNKS):
        for way in (0, 2):
            copy(tp, c, way, grad_ref).start()

        @pl.when(is_mid)
        def _():
            copy(tp, c, 1, grad_ref).start()

    @pl.when(mine < count - 1)
    def _():
        for which in range(3):
            halo_copy(which).start()

    mine_copy = pltpu.make_async_copy(grad_ref, got.at[tp], mine_sem)
    mine_copy.start()
    tile(tp, 0).start()

    @pl.when(mine == 0)
    def _():
        halo[...] = jnp.zeros_like(halo)

    @pl.when(mine > 0)
    def _():
        for which in range(3):
            halo_copy(which).wait_recv()

    groups = chan // LANES
    share = groups // CHUNKS

    def lanes(g):
        return pl.ds(pl.multiple_of(g * LANES, LANES), LANES)

    def first_part(c, carry):
        @pl.loop(0, share)
        def _(u):
            at = lanes(c * share + u)
            forward_ends(
                q_ref.at[:, at], k_ref.at[:, at], v_ref.at[:, at], halo.at[:, :, at],
                taps_ref.at[:, :, at], poles_ref.at[:, at], qs_ref.at[:, :, at],
                ks_ref.at[:, :, at], vs_ref.at[:, :, at], ends.at[:, :, at],
                own.at[0, :, at], wide,
            )

        copy(order[1], c, 0).wait_recv()

        @pl.when(is_mid | (c < half))
        def _():
            copy(order[1], c, 2).start()

        @pl.when(is_mid)
        def _():
            copy(order[1], c, 1).start()

        copy(order[2], c, 0).wait_recv()
        copy(order[2], c, 0).start()
        return carry

    lax.fori_loop(0, CHUNKS, first_part, 0)
    state_exchange(0, gathered)
    state_wait(0, gathered)

    def second_part(c, carry):
        @pl.loop(0, share)
        def _(u):
            at = lanes(c * share + u)
            forward_out(
                mine, ks_ref.at[:, :, at], vs_ref.at[:, :, at], ends.at[:, :, at],
                gathered.at[:, :, at], poles_ref.at[:, at], residues_ref.at[:, at],
                long_ref.at[:, :, at], starts,
            )

        copy(order[3], c, 0).wait_recv()
        copy(order[3], c, 2).start()

        @pl.when(is_mid)
        def _():
            copy(order[3], c, 1).start()

        return carry

    lax.fori_loop(0, CHUNKS, second_part, 0)
    mine_copy.wait()

    def multiply(k, carry):
        slot = pick(k)

        @pl.when(k == 4)
        def _():
            for c in range(CHUNKS):
                copy(order[4], c, 0).wait_recv()

                @pl.when(is_end)
                def _():
                    copy(order[4], c, 2).start()

                if c >= half:

                    @pl.when(is_mid)
                    def _():
                        copy(order[4], c, 1).start()

        @pl.when(k > 4)
        def _():
            for c in range(CHUNKS):
                copy(slot, c, 0).wait_recv()

        buffer = k % 2
        tile(slot, buffer).wait()

        @pl.when(k < 7)
        def _():
            tile(pick(k + 1), 1 - buffer).start()

        @pl.loop(0, chan // 256)
        def _(n):
            at = pl.ds(pl.multiple_of(n * 256, 256), 256)
            term = lax.dot_general(
                got[slot], tiles[buffer, at, :], (((1,), (1,)), ((), ())),
                preferred_element_type=F32,
            )

            @pl.when(k == 0)
            def _():
                mixed_ref[:, at] = term

            @pl.when(k > 0)
            def _():
                mixed_ref[:, at] += term

        return carry

    lax.fori_loop(0, 8, multiply, 0)

    @pl.loop(0, groups)
    def _(g):
        at = lanes(g)
        backward_ends(
            mixed_ref.at[:, at], qs_ref.at[:, :, at], poles_ref.at[:, at], back_ref.at[:, :, at],
            own.at[1, :, at], wide,
        )

    state_exchange(1, gathered_back_ref)
    for c in range(CHUNKS):
        copy(tp, c, 0, grad_ref).wait_send()
        copy(tp, c, 2, grad_ref).wait_send()
        copy(order[2], c, 0).wait_send()
        copy(order[3], c, 2).wait_send()

        @pl.when(is_mid | (c < half))
        def _():
            copy(order[1], c, 2).wait_send()

        @pl.when(is_end)
        def _():
            copy(order[4], c, 2).wait_send()

        @pl.when(is_mid)
        def _():
            copy(tp, c, 1, grad_ref).wait_send()
            copy(order[1], c, 1).wait_send()
            copy(order[3], c, 1).wait_send()
            if c >= half:
                copy(order[4], c, 1).wait_send()

    @pl.when(mine < count - 1)
    def _():
        for which in range(3):
            halo_copy(which).wait_send()

    state_wait(1, gathered_back_ref)


def lanes_spec(shape):
    lead = len(shape) - 1
    return pl.BlockSpec(tuple(shape[:-1]) + (LANES,), lambda g: (0,) * lead + (g,))


def call(body, inputs, outputs, scratch, flops, name, scalars=0):
    moved = sum(x.size * x.dtype.itemsize for x in list(inputs) + list(outputs))
    return pl.pallas_call(
        body,
        grid=(outputs[0].shape[-1] // LANES,),
        in_specs=[pl.BlockSpec(memory_space=pltpu.SMEM)] * scalars
        + [lanes_spec(x.shape) for x in inputs[scalars:]],
        out_specs=[lanes_spec(x.shape) for x in outputs],
        out_shape=list(outputs),
        scratch_shapes=scratch,
        cost_estimate=pl.CostEstimate(flops=flops, bytes_accessed=moved, transcendentals=0),
        compiler_params=pltpu.CompilerParams(vmem_limit_bytes=32 * 1024 * 1024),
        name=name,
    )(*inputs)


def shards(
    query_in, key_in, value_in, short_taps, modal_poles, modal_residues, out_weight, grad_out
):
    tap_count = short_taps.shape[1]
    rim = tap_count - 1
    tok_rows, chan = query_in.shape
    modes = modal_poles.shape[0]
    steps = tok_rows // SEGS
    mine = lax.axis_index("ctx").astype(jnp.int32)[None]
    sds = jax.ShapeDtypeStruct
    seg_shape = sds((steps, SEGS, chan), F32)
    state_shape = sds((modes, SEGS, chan), F32)
    own_shape = sds((modes, chan), F32)
    plain = sds((tok_rows, chan), jnp.bfloat16)
    rows_shape = sds((3, 8, chan), F32)
    work = tok_rows * chan
    count = lax.axis_size("ctx")
    if lax.axis_size("tp") == 8 and chan % (LANES * CHUNKS) == 0 and chan == grad_out.shape[1]:
        outputs = (
            sds((tok_rows, chan), F32), seg_shape, seg_shape, seg_shape, seg_shape, state_shape,
            sds((count, modes, chan), F32),
        )
        vmem = pl.BlockSpec(memory_space=pltpu.VMEM)
        hbm = pl.BlockSpec(memory_space=pl.ANY)
        dma = pltpu.SemaphoreType.DMA
        mixed, qs, ks, vs, long_out, ends, gathered = pl.pallas_call(
            gather_and_multiply,
            out_shape=outputs,
            in_specs=[hbm, hbm] + [vmem] * 6,
            out_specs=[vmem] * len(outputs),
            scratch_shapes=[
                pltpu.VMEM((8, tok_rows, grad_out.shape[1]), jnp.bfloat16),
                pltpu.VMEM((2, chan, grad_out.shape[1]), jnp.bfloat16),
                pltpu.VMEM((3, HALO, chan), jnp.bfloat16),
                pltpu.VMEM((tok_rows + HALO, LANES), F32),
                pltpu.VMEM((modes, SEGS, chan), F32),
                pltpu.VMEM((2, modes, chan), F32),
                pltpu.VMEM((count, modes, chan), F32),
                pltpu.VMEM((modes, SEGS, LANES), F32),
                dma((3, 8, CHUNKS)),
                dma((8, CHUNKS)),
                dma((2,)),
                dma,
                dma((3,)),
                dma((3,)),
                dma((2, count)),
                dma((2, count)),
            ],
            cost_estimate=pl.CostEstimate(
                flops=2 * work * out_weight.shape[1],
                bytes_accessed=2 * out_weight.size,
                transcendentals=0,
            ),
            compiler_params=pltpu.CompilerParams(
                collective_id=0, has_side_effects=True, vmem_limit_bytes=58 * 1024 * 1024
            ),
            name="gather_and_multiply",
        )(grad_out, out_weight, query_in, key_in, value_in, short_taps, modal_poles, modal_residues)
    else:
        gathered_out = lax.all_gather(grad_out, "tp", axis=1, tiled=True)
        last = jnp.stack([x[tok_rows - rim :] for x in (query_in, key_in, value_in)])
        prior = from_behind(last, "ctx", 1)
        prior = jnp.pad(prior, ((0, 0), (HALO - rim, 0), (0, 0)))
        qs, ks, vs, ends, own = call(
            forward_ends,
            (query_in, key_in, value_in, prior, short_taps, modal_poles),
            (seg_shape, seg_shape, seg_shape, state_shape, own_shape),
            [pltpu.VMEM((tok_rows + HALO, LANES), F32)],
            work * (3 * 2 * tap_count + 2 * modes),
            "forward_ends",
        )
        (long_out,) = call(
            lambda mine_ref, *refs: forward_out(mine_ref[0], *refs),
            (mine, ks, vs, ends, lax.all_gather(own, "ctx"), modal_poles, modal_residues),
            (seg_shape,),
            [pltpu.VMEM((modes, SEGS, LANES), F32)],
            work * 4 * modes,
            "forward_out",
            1,
        )
        mixed = lax.dot_general(
            gathered_out, out_weight, (((1,), (1,)), ((), ())), preferred_element_type=F32
        )
        ends, own = call(
            backward_ends,
            (mixed, qs, modal_poles),
            (state_shape, own_shape),
            [pltpu.VMEM((tok_rows, LANES), F32)],
            work * 2 * modes,
            "backward_ends",
        )
        gathered = lax.all_gather(own, "ctx")
    gated, gq, gk, gv, heads, tails = call(
        backward_out,
        (mine, mixed, qs, ks, vs, long_out, ends, gathered, short_taps,
         modal_poles, modal_residues),
        (plain, plain, plain, plain, rows_shape, rows_shape),
        [
            pltpu.VMEM((modes, SEGS, LANES), F32),
            pltpu.VMEM((3, steps, SEGS, LANES), F32),
            pltpu.VMEM((tok_rows, LANES), F32),
        ],
        work * (4 * modes + 6 * tap_count),
        "backward_out",
        1,
    )
    later = from_behind(heads, "ctx", -1)
    for j in range(1, tap_count):
        tails = tails.at[:, 8 - j :, :].add(short_taps[:, j, None, :] * later[:, :j, :])
    tails = tails.astype(jnp.bfloat16)
    grads = [
        lax.dynamic_update_slice(g, tails[i], (tok_rows - 8, 0)) for i, g in enumerate((gq, gk, gv))
    ]
    return (gated, *grads)


def solution(mesh):
    placed = (
        P("ctx", "tp"),
        P("ctx", "tp"),
        P("ctx", "tp"),
        P(None, None, "tp"),
        P(None, "tp"),
        P(None, "tp"),
        P("tp", None),
        P("ctx", "tp"),
    )
    return jax.shard_map(
        shards,
        mesh=mesh,
        in_specs=placed,
        out_specs=(P("ctx", "tp"), P("ctx", "tp"), P("ctx", "tp"), P("ctx", "tp")),
        check_vma=False,
    )
```

```python
import jax
import jax.numpy as jnp
from jax import lax
from jax.experimental import pallas as pl
from jax.experimental.pallas import tpu as pltpu
from jax.sharding import PartitionSpec as P

LANES = 128
SEGS = 8
UNROLL = 8
HALO = 16
CHUNKS = 4
MESH = pl.DeviceIdType.MESH
F32 = jnp.float32


def from_behind(block, axis, distance):
    devices = range(lax.axis_size(axis))
    route = [(i - distance, i) for i in devices if i - distance in devices]
    return lax.ppermute(block, axis, route)


def power(base, exponent):
    result = None
    while exponent:
        if exponent & 1:
            result = base if result is None else result * base
        exponent >>= 1
        if exponent:
            base = base * base
    return result


def spread(row):
    return jnp.broadcast_to(row, (SEGS, LANES))


def tree_sum(terms):
    while len(terms) > 1:
        paired = [a + b for a, b in zip(terms[::2], terms[1::2])]
        terms = paired + ([terms[-1]] if len(terms) % 2 else [])
    return terms[0]


def short_pass(load, store, taps, steps, history):
    def body(outer, past):
        past = list(past)
        for inner in range(UNROLL):
            step = outer * UNROLL + inner
            past = [load(step)] + past
            store(step, tree_sum([tap * row for tap, row in zip(taps, past)]))
            past = past[: len(taps) - 1]
        return tuple(past)

    lax.fori_loop(0, steps // UNROLL, body, tuple(history))


def forward_ends(
    q_ref, k_ref, v_ref, prior_ref, taps_ref, poles_ref,
    qs_ref, ks_ref, vs_ref, ends_ref, own_ref, wide,
):
    steps, tok_rows = qs_ref.shape[0], q_ref.shape[0]
    modes, tap_count = poles_ref.shape[0], taps_ref.shape[1]
    for which, (source, target) in enumerate(((q_ref, qs_ref), (k_ref, ks_ref), (v_ref, vs_ref))):
        wide[0:HALO, :] = prior_ref[which].astype(F32)
        wide[HALO : HALO + tok_rows, :] = source[...].astype(F32)
        taps = [spread(taps_ref[which, j : j + 1, :]) for j in range(tap_count)]

        def load(step):
            return wide[pl.ds(HALO + step, SEGS, stride=steps), :]

        def store(step, value, target=target):
            target[step] = value

        short_pass(load, store, taps, steps, [load(-1 - j) for j in range(tap_count - 1)])
    poles = [spread(poles_ref[m : m + 1, :]) for m in range(modes)]

    def body(outer, states):
        for inner in range(UNROLL):
            step = outer * UNROLL + inner
            row = ks_ref[step] * vs_ref[step]
            states = tuple(p * s + row for p, s in zip(poles, states))
        return states

    zero = jnp.zeros((SEGS, LANES), F32)
    states = lax.fori_loop(0, steps // UNROLL, body, (zero,) * modes)
    for m in range(modes):
        ends_ref[m] = states[m]
    seg_decay = power(poles_ref[...], steps)
    run = ends_ref[:, 0, :]
    for seg in range(1, SEGS):
        run = seg_decay * run + ends_ref[:, seg, :]
    own_ref[...] = run


def entering(mine, gathered_ref, ends_ref, poles_ref, starts, steps, backward):
    count = gathered_ref.shape[0]
    seg_decay = power(poles_ref[...], steps)
    block_decay = power(seg_decay, SEGS)
    run = jnp.zeros_like(seg_decay)
    order = range(count)
    for k in reversed(order) if backward else order:
        keep = (k > mine) if backward else (k < mine)
        run = jnp.where(keep, block_decay * run + gathered_ref[k], run)
    segs = range(SEGS)
    for seg in reversed(segs) if backward else segs:
        starts[:, seg, :] = run
        run = seg_decay * run + ends_ref[:, seg, :]


def forward_out(
    mine, ks_ref, vs_ref, ends_ref, gathered_ref, poles_ref, residues_ref, long_ref, starts,
):
    steps = ks_ref.shape[0]
    modes = poles_ref.shape[0]
    entering(mine, gathered_ref, ends_ref, poles_ref, starts, steps, False)
    poles = [spread(poles_ref[m : m + 1, :]) for m in range(modes)]
    residues = [spread(residues_ref[m : m + 1, :]) for m in range(modes)]

    def body(outer, states):
        for inner in range(UNROLL):
            step = outer * UNROLL + inner
            row = ks_ref[step] * vs_ref[step]
            states = tuple(p * s + row for p, s in zip(poles, states))
            out = tree_sum([r * s for r, s in zip(residues, states)])
            long_ref[step] = out
        return states

    lax.fori_loop(0, steps // UNROLL, body, tuple(starts[m] for m in range(modes)))


def backward_zero(
    base, mixed_ref, qs_ref, long_ref, poles_ref, residues_ref, states_ref, gq_ref, gp_ref,
):
    part = mixed_ref.shape[0] // SEGS
    modes = poles_ref.shape[0]
    poles = [spread(poles_ref[m : m + 1, :]) for m in range(modes)]
    residues = [spread(residues_ref[m : m + 1, :]) for m in range(modes)]

    def body(outer, states):
        for inner in range(UNROLL):
            place = part - 1 - (outer * UNROLL + inner)
            step = base + place
            mixed = mixed_ref[pl.ds(place, SEGS, stride=part), :]
            row = mixed * qs_ref[step]
            states = tuple(p * s + row for p, s in zip(poles, states))
            gq_ref[step] = mixed * long_ref[step]
            gp_ref[step] = tree_sum([r * s for r, s in zip(residues, states)])
        return states

    states = lax.fori_loop(
        0, part // UNROLL, body, tuple(states_ref[m] for m in range(modes))
    )
    for m in range(modes):
        states_ref[m] = states[m]


def backward_own(ends_ref, poles_ref, steps):
    seg_decay = power(poles_ref[...], steps)
    run = ends_ref[:, SEGS - 1, :]
    for seg in reversed(range(SEGS - 1)):
        run = seg_decay * run + ends_ref[:, seg, :]
    return run


def backward_whole(
    mixed_ref, qs_ref, long_ref, poles_ref, residues_ref, ends_ref, gq_ref, gp_ref, own_ref
):
    ends_ref[...] = jnp.zeros_like(ends_ref)
    backward_zero(
        0, mixed_ref, qs_ref, long_ref, poles_ref, residues_ref, ends_ref, gq_ref, gp_ref
    )
    own_ref[...] = backward_own(ends_ref, poles_ref, qs_ref.shape[0])


def backward_out(
    mine_ref, grad_q_ref, grad_p_ref, qs_ref, ks_ref, vs_ref, long_ref, ends_ref, gathered_ref,
    taps_ref, poles_ref, residues_ref,
    gated_ref, gq_ref, gk_ref, gv_ref, heads_ref, tails_ref, starts, grads, wide,
):
    steps, tok_rows = qs_ref.shape[0], gq_ref.shape[0]
    modes, tap_count = poles_ref.shape[0], taps_ref.shape[1]
    rim = tap_count - 1
    entering(mine_ref[0], gathered_ref, ends_ref, poles_ref, starts, steps, True)
    poles = [spread(poles_ref[m : m + 1, :]) for m in range(modes)]

    def body(outer, shares):
        for inner in range(UNROLL):
            step = steps - 1 - (outer * UNROLL + inner)
            shares = tuple(p * s for p, s in zip(poles, shares))
            out = grad_p_ref[step] + tree_sum(list(shares))
            grads[0, step] = out * vs_ref[step]
            grads[1, step] = out * ks_ref[step]
            wide[pl.ds(step, SEGS, stride=steps), :] = qs_ref[step] * long_ref[step]
        return shares

    lax.fori_loop(
        0, steps // UNROLL, body,
        tuple(spread(residues_ref[m : m + 1, :]) * starts[m] for m in range(modes)),
    )
    gated_ref[...] = wide[...].astype(jnp.bfloat16)
    zero_row = jnp.zeros((1, LANES), F32)
    sources = (grad_q_ref, grads.at[0], grads.at[1])
    for which, (source, target) in enumerate(zip(sources, (gq_ref, gk_ref, gv_ref))):
        heads_ref[which] = source[0:8, 0, :]
        later = [jnp.concatenate([source[j][1:], zero_row], axis=0) for j in range(rim)]
        taps = [spread(taps_ref[which, j : j + 1, :]) for j in range(tap_count)]

        def load(step, source=source):
            return source[steps - 1 - step]

        def store(step, value):
            wide[pl.ds(steps - 1 - step, SEGS, stride=steps), :] = value

        short_pass(load, store, taps, steps, later)
        tails_ref[which] = wide[tok_rows - 8 :, :]
        target[...] = wide[...].astype(jnp.bfloat16)


def own_plane(tp):
    z, x = tp // 2, tp % 2
    low = z < 2
    place = jnp.where(low, z, 3 - z)

    def shard(p, column):
        return jnp.where(low, p, 3 - p) * 2 + column

    return place, x, shard


def gather_and_multiply(
    grad_ref, weight_ref, q_in, k_in, v_in, taps_ref, poles_ref, residues_ref,
    gq_out, gp_out, qs_out, ks_out, vs_out, long_out, back_ref, gathered_back_ref,
    q_ref, k_ref, v_ref, mixed_ref, qs_ref, ks_ref, vs_ref, long_ref, got, tiles, halo, wide, ends, own, gathered, starts,
    send_sem, recv_sem, tile_sem, mine_sem, in_sem, out_sem, grad_sem, halo_send, halo_recv, state_send, state_recv,
):
    count = lax.axis_size("ctx")
    mine = lax.axis_index("ctx")
    tp = lax.axis_index("tp")
    place, x, shard = own_plane(tp)
    is_end = place == 0
    is_mid = place == 1
    tok_rows, chan = q_ref.shape
    steps, feat = grad_ref.shape[1:]
    part = steps // CHUNKS
    half = CHUNKS // 2
    inward, outward, across = shard(place + 1, x), shard(place - 1, x), shard(place, 1 - x)

    barrier = pltpu.get_barrier_semaphore()
    greeted = jnp.where(is_end, shard(3, x), outward)
    for peer in (inward, across, greeted):
        pl.semaphore_signal(barrier, inc=1, device_id={"tp": peer}, device_id_type=MESH)
    for gap in range(1, count):
        other = lax.rem(mine + gap, count)
        pl.semaphore_signal(barrier, inc=1, device_id={"ctx": other}, device_id_type=MESH)
    pl.semaphore_wait(barrier, count + 2)

    def rows(c):
        return pl.ds(pl.multiple_of((CHUNKS - 1 - c) * part, part), part)

    def copy(slot, c, way, source=None):
        piece = got.at[slot, :, rows(c), :]
        return pltpu.make_async_remote_copy(
            src_ref=piece if source is None else source.at[:, rows(c), :],
            dst_ref=piece,
            send_sem=send_sem.at[way, slot, c],
            recv_sem=recv_sem.at[slot, c],
            device_id={"tp": (inward, outward, across)[way]},
            device_id_type=MESH,
        )

    def tile(slot, buffer):
        columns = pl.ds(pl.multiple_of(slot * feat, feat), feat)
        return pltpu.make_async_copy(
            weight_ref.at[:, columns], tiles.at[buffer], tile_sem.at[buffer]
        )

    def halo_copy(which):
        source = (q_in, k_in, v_in)[which]
        return pltpu.make_async_remote_copy(
            src_ref=source.at[pl.ds(tok_rows - HALO, HALO), :],
            dst_ref=halo.at[which],
            send_sem=halo_send.at[which],
            recv_sem=halo_recv.at[which],
            device_id={"ctx": lax.rem(mine + 1, count)},
            device_id_type=MESH,
        )

    def state_copy(gap, way, landing):
        return pltpu.make_async_remote_copy(
            src_ref=own.at[way],
            dst_ref=landing.at[mine],
            send_sem=state_send.at[way, gap],
            recv_sem=state_recv.at[way, gap],
            device_id={"ctx": lax.rem(mine + gap, count)},
            device_id_type=MESH,
        )

    def state_exchange(way, landing):
        landing[mine] = own[way]
        for gap in range(1, count):
            state_copy(gap, way, landing).start()

    def state_wait(way, landing):
        for gap in range(1, count):
            state_copy(gap, way, landing).wait()

    def pair(k, end_slot, mid_slot):
        return jnp.where(is_end, end_slot, mid_slot)

    order = (
        tp,
        shard(place + 1, x),
        pair(2, shard(0, 1 - x), shard(0, x)),
        shard(place + 2, x),
        pair(4, shard(3, x), shard(1, 1 - x)),
        pair(5, shard(2, 1 - x), shard(0, 1 - x)),
        pair(6, shard(1, 1 - x), shard(2, 1 - x)),
        shard(3, 1 - x),
    )

    def pick(k):
        slot = order[7]
        for i in range(7):
            slot = jnp.where(k == i, order[i], slot)
        return slot

    for c in range(CHUNKS):
        for way in (0, 2):
            copy(tp, c, way, grad_ref).start()

        @pl.when(is_mid)
        def _():
            copy(tp, c, 1, grad_ref).start()

    ins = [
        pltpu.make_async_copy(source, target, in_sem.at[i])
        for i, (source, target) in enumerate(((q_in, q_ref), (k_in, k_ref), (v_in, v_ref)))
    ]
    outs = [
        pltpu.make_async_copy(source, target, out_sem.at[i])
        for i, (source, target) in enumerate(
            (
                (qs_ref, qs_out), (ks_ref, ks_out), (vs_ref, vs_out), (long_ref, long_out),
            )
        )
    ]
    for each in ins:
        each.start()

    @pl.when(mine < count - 1)
    def _():
        for which in range(3):
            halo_copy(which).start()

    mine_copy = pltpu.make_async_copy(grad_ref, got.at[tp], mine_sem)
    mine_copy.start()
    tile(tp, 0).start()

    @pl.when(mine == 0)
    def _():
        halo[...] = jnp.zeros_like(halo)

    @pl.when(mine > 0)
    def _():
        for which in range(3):
            halo_copy(which).wait_recv()

    for each in ins:
        each.wait()
    groups = chan // LANES
    share = groups // CHUNKS

    def lanes(g):
        return pl.ds(pl.multiple_of(g * LANES, LANES), LANES)

    def first_part(c, carry):
        @pl.loop(0, share)
        def _(u):
            at = lanes(c * share + u)
            forward_ends(
                q_ref.at[:, at], k_ref.at[:, at], v_ref.at[:, at], halo.at[:, :, at],
                taps_ref.at[:, :, at], poles_ref.at[:, at], qs_ref.at[:, :, at],
                ks_ref.at[:, :, at], vs_ref.at[:, :, at], ends.at[:, :, at],
                own.at[0, :, at], wide,
            )

        copy(order[1], c, 0).wait_recv()

        @pl.when(is_mid | (c < half))
        def _():
            copy(order[1], c, 2).start()

        @pl.when(is_mid)
        def _():
            copy(order[1], c, 1).start()

        copy(order[2], c, 0).wait_recv()
        copy(order[2], c, 0).start()
        return carry

    lax.fori_loop(0, CHUNKS, first_part, 0)
    for each in outs[:3]:
        each.start()
    state_exchange(0, gathered)
    state_wait(0, gathered)

    def second_part(c, carry):
        @pl.loop(0, share)
        def _(u):
            at = lanes(c * share + u)
            forward_out(
                mine, ks_ref.at[:, :, at], vs_ref.at[:, :, at], ends.at[:, :, at],
                gathered.at[:, :, at], poles_ref.at[:, at], residues_ref.at[:, at],
                long_ref.at[:, :, at], starts,
            )

        copy(order[3], c, 0).wait_recv()
        copy(order[3], c, 2).start()

        @pl.when(is_mid)
        def _():
            copy(order[3], c, 1).start()

        return carry

    lax.fori_loop(0, CHUNKS, second_part, 0)
    outs[3].start()
    mine_copy.wait()

    def product(slot, c, buffer):
        term = lax.dot_general(
            got[slot, :, rows(c), :].reshape(SEGS * part, feat), tiles[buffer],
            (((1,), (1,)), ((), ())), preferred_element_type=F32,
        )
        return term.reshape(SEGS, part, chan)

    def multiply(k, carry):
        slot = pick(k)

        @pl.when(k == 4)
        def _():
            for c in range(CHUNKS):
                copy(order[4], c, 0).wait_recv()

                @pl.when(is_end)
                def _():
                    copy(order[4], c, 2).start()

                if c >= half:

                    @pl.when(is_mid)
                    def _():
                        copy(order[4], c, 1).start()

        buffer = k % 2
        tile(slot, buffer).wait()

        tile(pick(k + 1), 1 - buffer).start()

        @pl.loop(0, CHUNKS)
        def _(c):
            @pl.when(k > 4)
            def _():
                copy(slot, c, 0).wait_recv()

            at = rows(c)
            term = product(slot, c, buffer)

            @pl.when(k == 0)
            def _():
                mixed_ref[:, at, :] = term

            @pl.when(k > 0)
            def _():
                mixed_ref[:, at, :] += term

        return carry

    lax.fori_loop(0, 6, multiply, 0)
    tile(order[7], 1).start()
    for each in outs[1:3]:
        each.wait()
    gq_ref, gp_ref = ks_ref, vs_ref
    back_ref[...] = jnp.zeros_like(back_ref)
    tile(order[6], 0).wait()
    tile(order[7], 1).wait()

    def grad_copy(which, c):
        source, target = ((gq_ref, gq_out), (gp_ref, gp_out))[which]
        return pltpu.make_async_copy(
            source.at[rows(c)], target.at[rows(c)], grad_sem.at[which, c]
        )

    def last_part(c, carry):
        for i in (6, 7):
            copy(order[i], c, 0).wait_recv()
            mixed_ref[:, rows(c), :] += product(order[i], c, i - 6)
        chunk = wide.at[0 : SEGS * part, :]

        @pl.loop(0, groups)
        def _(g):
            at = lanes(g)
            for seg in range(SEGS):
                wide[seg * part : (seg + 1) * part, :] = mixed_ref[seg, rows(c), at]
            backward_zero(
                (CHUNKS - 1 - c) * part, chunk, qs_ref.at[:, :, at], long_ref.at[:, :, at],
                poles_ref.at[:, at], residues_ref.at[:, at], back_ref.at[:, :, at],
                gq_ref.at[:, :, at], gp_ref.at[:, :, at],
            )

        for which in range(2):
            grad_copy(which, c).start()
        return carry

    lax.fori_loop(0, CHUNKS, last_part, 0)
    own[1] = backward_own(back_ref, poles_ref, steps)
    state_exchange(1, gathered_back_ref)
    for c in range(CHUNKS):
        copy(tp, c, 0, grad_ref).wait_send()
        copy(tp, c, 2, grad_ref).wait_send()
        copy(order[2], c, 0).wait_send()
        copy(order[3], c, 2).wait_send()

        @pl.when(is_mid | (c < half))
        def _():
            copy(order[1], c, 2).wait_send()

        @pl.when(is_end)
        def _():
            copy(order[4], c, 2).wait_send()

        @pl.when(is_mid)
        def _():
            copy(tp, c, 1, grad_ref).wait_send()
            copy(order[1], c, 1).wait_send()
            copy(order[3], c, 1).wait_send()
            if c >= half:
                copy(order[4], c, 1).wait_send()

    @pl.when(mine < count - 1)
    def _():
        for which in range(3):
            halo_copy(which).wait_send()

    state_wait(1, gathered_back_ref)
    for each in (outs[0], outs[3]):
        each.wait()
    for which in range(2):
        for c in range(CHUNKS):
            grad_copy(which, c).wait()


def lanes_spec(shape):
    lead = len(shape) - 1
    return pl.BlockSpec(tuple(shape[:-1]) + (LANES,), lambda g: (0,) * lead + (g,))


def call(body, inputs, outputs, scratch, flops, name, scalars=0, room=32):
    moved = sum(x.size * x.dtype.itemsize for x in list(inputs) + list(outputs))
    return pl.pallas_call(
        body,
        grid=(outputs[0].shape[-1] // LANES,),
        in_specs=[pl.BlockSpec(memory_space=pltpu.SMEM)] * scalars
        + [lanes_spec(x.shape) for x in inputs[scalars:]],
        out_specs=[lanes_spec(x.shape) for x in outputs],
        out_shape=list(outputs),
        scratch_shapes=scratch,
        cost_estimate=pl.CostEstimate(flops=flops, bytes_accessed=moved, transcendentals=0),
        compiler_params=pltpu.CompilerParams(vmem_limit_bytes=room * 1024 * 1024),
        name=name,
    )(*inputs)


def shards(
    query_in, key_in, value_in, short_taps, modal_poles, modal_residues, out_weight, grad_out
):
    tap_count = short_taps.shape[1]
    rim = tap_count - 1
    tok_rows, chan = query_in.shape
    modes = modal_poles.shape[0]
    steps = tok_rows // SEGS
    mine = lax.axis_index("ctx").astype(jnp.int32)[None]
    sds = jax.ShapeDtypeStruct
    seg_shape = sds((steps, SEGS, chan), F32)
    state_shape = sds((modes, SEGS, chan), F32)
    own_shape = sds((modes, chan), F32)
    plain = sds((tok_rows, chan), jnp.bfloat16)
    rows_shape = sds((3, 8, chan), F32)
    work = tok_rows * chan
    count = lax.axis_size("ctx")
    if lax.axis_size("tp") == 8 and chan % (LANES * CHUNKS) == 0 and chan == grad_out.shape[1]:
        outputs = (
            seg_shape, seg_shape, seg_shape, seg_shape, seg_shape, seg_shape, state_shape,
            sds((count, modes, chan), F32),
        )
        vmem = pl.BlockSpec(memory_space=pltpu.VMEM)
        hbm = pl.BlockSpec(memory_space=pl.ANY)
        dma = pltpu.SemaphoreType.DMA
        gq, gp, qs, ks, vs, long_out, ends, gathered = pl.pallas_call(
            gather_and_multiply,
            out_shape=outputs,
            in_specs=[hbm] * 5 + [vmem] * 3,
            out_specs=[hbm] * 6 + [vmem] * 2,
            scratch_shapes=[pltpu.VMEM((tok_rows, chan), jnp.bfloat16)] * 3
            + [pltpu.VMEM((SEGS, steps, chan), F32)]
            + [pltpu.VMEM(seg_shape.shape, F32)] * 4
            + [
                pltpu.VMEM((8, SEGS, steps, grad_out.shape[1]), jnp.bfloat16),
                pltpu.VMEM((2, chan, grad_out.shape[1]), jnp.bfloat16),
                pltpu.VMEM((3, HALO, chan), jnp.bfloat16),
                pltpu.VMEM((tok_rows + HALO, LANES), F32),
                pltpu.VMEM((modes, SEGS, chan), F32),
                pltpu.VMEM((2, modes, chan), F32),
                pltpu.VMEM((count, modes, chan), F32),
                pltpu.VMEM((modes, SEGS, LANES), F32),
                dma((3, 8, CHUNKS)),
                dma((8, CHUNKS)),
                dma((2,)),
                dma,
                dma((3,)),
                dma((4,)),
                dma((2, CHUNKS)),
                dma((3,)),
                dma((3,)),
                dma((2, count)),
                dma((2, count)),
            ],
            cost_estimate=pl.CostEstimate(
                flops=2 * work * out_weight.shape[1],
                bytes_accessed=2 * out_weight.size,
                transcendentals=0,
            ),
            compiler_params=pltpu.CompilerParams(
                collective_id=0, has_side_effects=True, vmem_limit_bytes=58 * 1024 * 1024
            ),
            name="gather_and_multiply",
        )(grad_out.reshape(SEGS, steps, -1), out_weight, query_in, key_in, value_in, short_taps, modal_poles, modal_residues)
    else:
        gathered_out = lax.all_gather(grad_out, "tp", axis=1, tiled=True)
        last = jnp.stack([x[tok_rows - rim :] for x in (query_in, key_in, value_in)])
        prior = from_behind(last, "ctx", 1)
        prior = jnp.pad(prior, ((0, 0), (HALO - rim, 0), (0, 0)))
        qs, ks, vs, ends, own = call(
            forward_ends,
            (query_in, key_in, value_in, prior, short_taps, modal_poles),
            (seg_shape, seg_shape, seg_shape, state_shape, own_shape),
            [pltpu.VMEM((tok_rows + HALO, LANES), F32)],
            work * (3 * 2 * tap_count + 2 * modes),
            "forward_ends",
        )
        (long_out,) = call(
            lambda mine_ref, *refs: forward_out(mine_ref[0], *refs),
            (mine, ks, vs, ends, lax.all_gather(own, "ctx"), modal_poles, modal_residues),
            (seg_shape,),
            [pltpu.VMEM((modes, SEGS, LANES), F32)],
            work * 4 * modes,
            "forward_out",
            1,
        )
        mixed = lax.dot_general(
            gathered_out, out_weight, (((1,), (1,)), ((), ())), preferred_element_type=F32
        )
        ends, gq, gp, own = call(
            backward_whole,
            (mixed, qs, long_out, modal_poles, modal_residues),
            (state_shape, seg_shape, seg_shape, own_shape),
            [],
            work * 4 * modes,
            "backward_whole",
        )
        gathered = lax.all_gather(own, "ctx")
    gated, gq, gk, gv, heads, tails = call(
        backward_out,
        (mine, gq, gp, qs, ks, vs, long_out, ends, gathered, short_taps,
         modal_poles, modal_residues),
        (plain, plain, plain, plain, rows_shape, rows_shape),
        [
            pltpu.VMEM((modes, SEGS, LANES), F32),
            pltpu.VMEM((2, steps, SEGS, LANES), F32),
            pltpu.VMEM((tok_rows, LANES), F32),
        ],
        work * (2 * modes + 6 * tap_count),
        "backward_out",
        1,
        60,
    )
    later = from_behind(heads, "ctx", -1)
    beyond = jnp.pad(later, ((0, 0), (8, 0), (0, 0)))
    for j in range(1, tap_count):
        tails = tails + short_taps[:, j, None, :] * beyond[:, j : j + 8, :]
    tails = tails.astype(jnp.bfloat16)
    grads = [
        lax.dynamic_update_slice(g, tails[i], (tok_rows - 8, 0)) for i, g in enumerate((gq, gk, gv))
    ]
    return (gated, *grads)


def solution(mesh):
    placed = (
        P("ctx", "tp"),
        P("ctx", "tp"),
        P("ctx", "tp"),
        P(None, None, "tp"),
        P(None, "tp"),
        P(None, "tp"),
        P("tp", None),
        P("ctx", "tp"),
    )
    return jax.shard_map(
        shards,
        mesh=mesh,
        in_specs=placed,
        out_specs=(P("ctx", "tp"), P("ctx", "tp"), P("ctx", "tp"), P("ctx", "tp")),
        check_vma=False,
    )
```
